512 devices in a mesh: tok: 2 (over core), ein: 8 (over y_lo, x), eout: 32 (over y_hi, z).
Axes of the slice: x: 4, y: 8 (y_hi: 4, y_lo: 2; y = y_hi * 2 + y_lo), z: 8, core: 2. Of those that a mesh axis runs over, the one named last changes fastest.
Arguments:
- activations: bfloat16 [1024, 28672], P(('tok', 'ein'), 'eout'), may hold values from -6 to 6
- gradients: bfloat16 [1024, 8192], P('eout', ('tok', 'ein')), may hold values from -0.375 to 0.375
- in_basis: bfloat16 [28672, 14336], P('eout', ('tok', 'ein')), may hold values from -0.03125 to 0.03125
- out_basis: bfloat16 [8192, 8192], P(('tok', 'ein'), 'eout'), may hold values from -0.0625 to 0.0625
- example_ids: int32 [1024], replicated, may hold values from 0 to 3, never falling along the last dimension, each value on 1 to 512 neighbouring positions
Outputs:
- scaling: float32 [14336, 8192], P(('tok', 'ein'), 'eout')
The draws below stay inside these ranges and needn't reach their ends.
Inputs may be any that keep to these rules, and one draw needn't show every extreme that they name: `example_ids`: each example's tokens form one contiguous run, examples in increasing order; every example has at least one token and one example has exactly 512.
All inputs are finite; a program needn't handle non-finite values.
Results may differ from the reference program's by a relative error of at most 0.0039.
Values may be sent and summed in bfloat16 or wider, within the bound.
A program may use at most 64 MiB of HBM per device.

```python
import math
import jax
import jax.numpy as jnp
import numpy as np
from jax import lax

DIN = 28672
DOUT = 8192
KIN = 14336
EXAMPLES = 4
TOKENS = 1024


def block_scale(stream_key, dims, cuts, least, largest):
    level = 1.0
    for position, parts in cuts:
        steps = jax.random.uniform(jax.random.fold_in(jax.random.fold_in(stream_key, 6), position), (parts,), jnp.float32, least / len(cuts), largest / len(cuts))
        level = level * jnp.repeat(jnp.exp(steps), dims[position] // parts).reshape((-1,) + (1,) * (len(dims) - 1 - position))
    return level


def split_up(count, total, bound, lean):
    weights = [(1 << 20) // math.isqrt(standing ** lean) + 1 for standing in range(2, count + 1)]
    rest, holding = total - bound - (count - 1), [1] * (count - 1)
    while rest > 0:
        candidates = [i for i in range(count - 1) if holding[i] < bound]
        pool, left = sum([weights[i] for i in candidates]), rest
        for i in candidates:
            addition = min(bound - holding[i], max(1, left * weights[i] // pool), rest)
            holding[i] = holding[i] + addition
            rest = rest - addition
    return np.array([bound] + holding)


def uneven_parts(stream_key, count, total, most, skew):
    if count == 2:
        one = jax.random.randint(stream_key, (), max(1, total - most), min(most, total - 1) + 1)
        return jnp.stack([one, total - one])
    lengths = jnp.asarray(split_up(count, total, most, skew), jnp.int32)
    twos = (count - 1) // 2
    giver, receiver = lengths[1:1 + 2 * twos:2], lengths[2:2 + 2 * twos:2]
    margin = jnp.minimum(giver - 1, most - receiver)
    moved = jax.random.randint(jax.random.fold_in(stream_key, 1), (twos,), 0, 1 << 20) % (margin + 1)
    lengths = lengths.at[1:1 + 2 * twos:2].set(giver - moved).at[2:2 + 2 * twos:2].set(receiver + moved)
    return lengths[jax.random.permutation(jax.random.fold_in(stream_key, 2), count)]


def bell_draw(key, shape, scale, reach, split=(), held_as=jnp.bfloat16):
    drawn = scale * jax.random.normal(key, shape, jnp.float32)
    if split:
        drawn = drawn * block_scale(key, shape, split, -0.22, 0.18)
    return jnp.clip(drawn, -reach, reach).astype(held_as)


def setup_inputs(seed: int = 0) -> dict:
    keys = jax.random.split(jax.random.key(seed), 6)
    return {
        "activations": bell_draw(keys[0], (TOKENS, DIN), 1.0, 6.0, ((0, 16), (1, 32))),
        "gradients": bell_draw(keys[1], (TOKENS, DOUT), ((TOKENS // EXAMPLES) ** -0.5), 0.375, ((0, 32), (1, 16))),
        "in_basis": bell_draw(keys[2], (DIN, KIN), DIN ** -0.5, 0.03125, ((0, 32), (1, 16))),
        "out_basis": bell_draw(keys[3], (DOUT, DOUT), DOUT ** -0.5, 0.0625, ((0, 16), (1, 32))),
        "example_ids": jnp.searchsorted(jnp.cumsum(uneven_parts(keys[4], EXAMPLES, TOKENS, TOKENS // 2, 0)), jnp.arange(TOKENS), side="right").astype(jnp.int32),
    }


def reference(activations, gradients, in_basis, out_basis, example_ids):
    rotated_in = jnp.dot(activations, in_basis, preferred_element_type=jnp.float32).astype(jnp.bfloat16)
    rotated_out = jnp.dot(gradients, out_basis, preferred_element_type=jnp.float32).astype(jnp.bfloat16)
    transposed = rotated_in.T

    def accumulate(total, index):
        keeper = (example_ids == index).astype(rotated_out.dtype)
        tile = jnp.dot(transposed, rotated_out * keeper[:, None], preferred_element_type=jnp.float32)
        return total + tile * tile, None

    total, _ = lax.scan(accumulate, jnp.zeros((KIN, DOUT), jnp.float32), jnp.arange(EXAMPLES, dtype=jnp.int32))
    return total / EXAMPLES
```

```python
import jax
import jax.numpy as jnp
from jax import lax
from jax.experimental import pallas as pl
from jax.experimental.pallas import tpu as pltpu
from jax.sharding import PartitionSpec as P

EXAMPLES = 4
F32, BF16 = jnp.float32, jnp.bfloat16
MESH = pl.DeviceIdType.MESH
X, YL, YH, Z = 4, 2, 4, 8

WIDTHS = (256, 256, 256, 128)
HOPS = ((4, 3), (3, 4), (3, 4), (4, 3))
STARTS = (0, 256, 512, 768)
PARTS = len(WIDTHS)
GRAD_HOPS = ((4, 3), (3, 4), (3, 4), (4, 3))
SIGN = (1, -1)

ORDER = (
    ("s",), ("g", 0, 1), ("gy", 3), ("f", 1), ("f", 2), ("f", 3), ("g", 0, 2), ("gy", 1), ("g", 1, 1), ("f", 4),
    ("m", 0), ("gy", 2), ("m", 2), ("g", 0, 3), ("f", 5), ("f", 6), ("g", 3, 1), ("g", 1, 2), ("g", 2, 1), ("f", 7),
    ("m", 1), ("g", 0, 4), ("g", 3, 2), ("m", 3), ("r", 0, 0), ("g", 1, 3), ("g", 2, 2), ("g", 3, 3), ("r", 0, 1),
    ("g", 1, 4), ("g", 2, 3), ("g", 3, 4), ("r", 0, 2), ("r", 2, 0), ("g", 2, 4), ("o",), ("r", 1, 0), ("r", 0, 3),
    ("c1",), ("r", 2, 1), ("r", 3, 0), ("r", 1, 1), ("rf", 0), ("r", 2, 2), ("r", 3, 1), ("r", 1, 2), ("c2",),
    ("r", 2, 3), ("r", 3, 2), ("r", 1, 3), ("y", 0), ("c3", 4), ("c3", 1), ("r", 3, 3), ("c3", 2), ("c3", 3),
    ("rf", 2), ("c3", 5), ("c3", 7), ("c3", 6), ("rf", 1), ("a", 0, 0), ("rf", 3), ("c4",), ("y", 2), ("a", 0, 1),
    ("y", 1), ("y", 3), ("a", 0, 2), ("a", 2, 0), ("a", 1, 0), ("a", 3, 0), ("a", 0, 3), ("a", 2, 1), ("a", 1, 1),
    ("a", 3, 1), ("af", 0), ("a", 2, 2), ("a", 1, 2), ("a", 3, 2), ("a", 2, 3), ("a", 1, 3), ("a", 3, 3), ("af", 2),
    ("af", 3), ("af", 1),
)

MESSAGES = (
    [("f", i) for i in range(1, 8)]
    + [("k", i) for i in range(8)]
    + [("gy", k) for k in range(1, 4)]
    + [("g", r, d, s) for r in range(4) for d in range(2) for s in range(GRAD_HOPS[r][d])]
    + [("sw",)]
    + [("d", j) for j in range(1, 8)]
    + [("cg", j) for j in range(1, 8)]
    + [("ck", j) for j in range(8)]
    + [("r", p, d, s) for p in range(PARTS) for d in range(2) for s in range(HOPS[p][d])]
    + [("yr", p, k) for p in range(PARTS) for k in range(1, 4)]
    + [("ya", p, k) for p in range(PARTS) for k in range(1, 4)]
    + [("a", p, d, s) for p in range(PARTS) for d in range(2) for s in range(HOPS[p][d])]
)
NUMBER = {name: i for i, name in enumerate(MESSAGES)}
LAG = 12


def rows(start, size):
    return pl.ds(pl.multiple_of(start, size), size)


def kernel(ids, act, grad, wi_hbm, wo_hbm, out_hbm, A, W, G, WO, PO, PR, PS, PQ, RO, MT, OUT, *rest):
    PI, R, YS = rest[0:PARTS], rest[PARTS : 2 * PARTS], rest[2 * PARTS : 3 * PARTS]
    YR, ZS, ZR = rest[3 * PARTS : 4 * PARTS], rest[4 * PARTS : 5 * PARTS], rest[5 * PARTS : 6 * PARTS]
    send_sem, recv_sem, local_sem = rest[6 * PARTS :]

    c = lax.axis_index("tok")
    e = lax.axis_index("ein")
    o = lax.axis_index("eout")
    x, yl = e % X, e // X
    z, yh = o % Z, o // Z

    def dev(dx=0, dyl=0, dyh=0, dz=0, dc=0):
        return (
            (c + dc) % 2,
            (yl + dyl) % YL * X + (x + dx) % X,
            (yh + dyh) % YH * Z + (z + dz) % Z,
        )

    def te(dx=0, dyl=0, dc=0):
        return (c + dc) % 2 * 8 + (yl + dyl) % YL * X + (x + dx) % X

    load_wi = pltpu.make_async_copy(wi_hbm, W, local_sem.at[0])
    load_wo = pltpu.make_async_copy(wo_hbm, WO, local_sem.at[1])
    load_wi.start()
    load_wo.start()

    barrier = pltpu.get_barrier_semaphore()
    partners = [dev(dc=1), dev(dz=1), dev(dz=-1)]
    partners += [dev(dyh=k) for k in range(1, YH)]
    partners += [dev(dx=j % 4, dyl=j // 4) for j in range(1, 8)]
    for partner in partners:
        pl.semaphore_signal(barrier, 1, device_id=partner, device_id_type=MESH)
    pl.semaphore_wait(barrier, len(partners))

    flying = {}
    unsent = []
    step_number = [0]

    def send(name, src, dst, to):
        m = NUMBER[name]
        copy = pltpu.make_async_remote_copy(
            src_ref=src,
            dst_ref=dst,
            send_sem=send_sem.at[m],
            recv_sem=recv_sem.at[m],
            device_id=to,
            device_id_type=MESH,
        )
        copy.start()
        flying[name] = copy
        unsent.append((step_number[0], copy))

    def arrived(name):
        flying.pop(name).wait_recv()

    block_of = {
        0: te(), 1: te(dyl=1), 2: te(dx=-1), 3: te(dx=1), 4: te(dx=2),
        5: te(dx=-1, dyl=1), 6: te(dx=1, dyl=1), 7: te(dx=2, dyl=1),
    }

    def to_other_core(i):
        b = block_of[i]
        src = act if i == 0 else A.at[b]
        send(("k", i), src, A.at[b], dev(dc=1))

    def step_s():
        mine = A.at[te()]
        send(("f", 1), act, mine, dev(dyl=1))
        send(("f", 2), act, mine, dev(dx=1))
        send(("f", 3), act, mine, dev(dx=-1))
        send(("f", 4), act, mine, dev(dx=2))
        for d in (0, 1):
            send(("g", 0, d, 0), grad, G.at[o], dev(dz=SIGN[d]))
        for k in (1, 3, 2):
            send(("gy", k), grad, G.at[o], dev(dyh=k))
        to_other_core(0)
        A[te()] = act[...]
        G[o] = grad[...]

    def step_f(i):
        arrived(("f", i))
        if i == 1:
            b = A.at[block_of[1]]
            send(("f", 5), b, b, dev(dx=1))
            send(("f", 6), b, b, dev(dx=-1))
        if i == 4:
            b = A.at[block_of[4]]
            send(("f", 7), b, b, dev(dyl=1))
        to_other_core(i)

    def step_m(g):
        if g == 0:
            load_wi.wait()
        for i in ((), (), (0, 2, 3, 4), (1, 5, 6, 7))[g]:
            arrived(("k", i))
        group = (c + g // 2) % 2 * 2 + (yl + g % 2) % 2
        lhs = A[pl.ds(group * 4, 4)].reshape(256, 896)
        for p in range(PARTS):
            PI[p][rows(group * 256, 256), :] = jnp.dot(
                lhs, W[:, STARTS[p] : STARTS[p] + WIDTHS[p]], preferred_element_type=F32
            )

    def send_gradient(r, d, s):
        b = G.at[(yh + r) % YH * Z + (z - SIGN[d] * s) % Z]
        send(("g", r, d, s), b, b, dev(dz=SIGN[d]))

    def step_gy(k):
        arrived(("gy", k))
        for d in (0, 1):
            send_gradient(YH - k, d, 0)

    def step_g(r, s):
        for d in (0, 1):
            if s <= GRAD_HOPS[r][d]:
                arrived(("g", r, d, s - 1))
            if s < GRAD_HOPS[r][d]:
                send_gradient(r, d, s)

    def step_o():
        load_wo.wait()
        for h in range(4):
            PO[h * 256 : (h + 1) * 256, :] = jnp.dot(
                G[h * 8 : (h + 1) * 8].reshape(256, 512), WO[...], preferred_element_type=F32
            )
        send(("sw",), PO.at[rows((1 - c) * 512, 512)], PR, dev(dc=1))

    def step_c1():
        arrived(("sw",))
        PS[...] = PO[rows(c * 512, 512), :] + PR[...]
        for j in (4, 1, 3, 2, 5, 7, 6):
            to = (yl + j // 4) % YL * X + (x + j % 4) % X
            send(("d", j), PS.at[rows(to * 64, 64)], PQ.at[j], dev(dx=j % 4, dyl=j // 4))

    def step_c2():
        total = PS[rows(e * 64, 64), :]
        for j in range(1, 8):
            arrived(("d", j))
            total = total + PQ[j]
        mine = rows(te() * 64, 64)
        RO[mine, :] = total.astype(BF16)
        for j in (4, 1, 3, 2, 5, 7, 6):
            send(("cg", j), RO.at[mine], RO.at[mine], dev(dx=j % 4, dyl=j // 4))
        send(("ck", 0), RO.at[mine], RO.at[mine], dev(dc=1))

    def step_c3(j):
        arrived(("cg", j))
        b = RO.at[rows(te(dx=-(j % 4), dyl=j // 4) * 64, 64)]
        send(("ck", j), b, b, dev(dc=1))

    def step_c4():
        for j in range(8):
            arrived(("ck", j))
        for t in range(8):
            columns = slice(t * 128, (t + 1) * 128)
            block = RO[columns, :].astype(F32).T
            for n in range(EXAMPLES):
                MT[n * 256 : (n + 1) * 256, columns] = jnp.where(
                    ids[t : t + 1, :] == n, block, 0.0
                ).astype(BF16)

    def step_r(p, s):
        for d in (0, 1):
            hops = HOPS[p][d]
            if s >= hops:
                continue
            chunk = rows((z + SIGN[d] * (hops - s)) % Z * 128, 128)
            value = PI[p][chunk, :]
            if s > 0:
                arrived(("r", p, d, s - 1))
                value = value + ZR[p][d * 4 + s - 1].astype(F32)
            ZS[p][d * 4 + s] = value.astype(BF16)
            send(("r", p, d, s), ZS[p].at[d * 4 + s], ZR[p].at[d * 4 + s], dev(dz=SIGN[d]))

    def step_rf(p):
        value = PI[p][rows(z * 128, 128), :]
        for d in (0, 1):
            last = HOPS[p][d] - 1
            arrived(("r", p, d, last))
            value = value + ZR[p][d * 4 + last].astype(F32)
        YS[p][...] = value
        for k in (1, 3, 2):
            send(("yr", p, k), YS[p].at[rows((yh + k) % YH * 32, 32)], YR[p].at[k], dev(dyh=k))

    def step_y(p):
        value = YS[p][rows(yh * 32, 32), :]
        for k in (1, 2, 3):
            arrived(("yr", p, k))
            value = value + YR[p][k]
        mine = rows(o_row() * 32, 32)
        R[p][mine, :] = value.astype(BF16)
        for k in (1, 3, 2):
            send(("ya", p, k), R[p].at[mine], R[p].at[mine], dev(dyh=k))

    def o_row():
        return z * YH + yh

    def step_a(p, s):
        if s == 0:
            for k in (1, 2, 3):
                arrived(("ya", p, k))
        for d in (0, 1):
            hops = HOPS[p][d]
            if s >= hops:
                continue
            if s > 0:
                arrived(("a", p, d, s - 1))
            b = R[p].at[rows((z - SIGN[d] * s) % Z * 128, 128)]
            send(("a", p, d, s), b, b, dev(dz=SIGN[d]))

    def step_af(p):
        for d in (0, 1):
            arrived(("a", p, d, HOPS[p][d] - 1))
        total = None
        for n in range(EXAMPLES):
            tile = jnp.dot(MT[n * 256 : (n + 1) * 256, :], R[p][...], preferred_element_type=F32)
            total = tile * tile if total is None else total + tile * tile
        here = slice(STARTS[p], STARTS[p] + WIDTHS[p])
        OUT[here, :] = total.T
        copy = pltpu.make_async_copy(OUT.at[here], out_hbm.at[here], local_sem.at[2 + p])
        copy.start()
        stores.append(copy)

    stores = []
    steps = {
        "s": step_s, "f": step_f, "m": step_m, "gy": step_gy, "g": step_g, "o": step_o, "c1": step_c1, "c2": step_c2,
        "c3": step_c3, "c4": step_c4, "r": step_r, "rf": step_rf, "y": step_y, "a": step_a, "af": step_af,
    }
    for name, *which in ORDER:
        steps[name](*which)
        step_number[0] += 1
        while unsent and unsent[0][0] < step_number[0] - LAG:
            unsent.pop(0)[1].wait_send()
    for _, copy in unsent:
        copy.wait_send()
    for copy in stores:
        copy.wait()


def shards(activations, gradients, in_basis, out_basis, example_ids):
    vmem, anywhere = pl.BlockSpec(memory_space=pltpu.VMEM), pl.BlockSpec(memory_space=pl.ANY)
    squares = pl.pallas_call(
        kernel,
        out_shape=jax.ShapeDtypeStruct((896, 256), F32),
        in_specs=[vmem, vmem, vmem, anywhere, anywhere],
        out_specs=anywhere,
        scratch_shapes=[
            pltpu.VMEM((16, 64, 896), BF16),
            pltpu.VMEM((896, 896), BF16),
            pltpu.VMEM((32, 32, 512), BF16),
            pltpu.VMEM((512, 256), BF16),
            pltpu.VMEM((1024, 256), F32),
            pltpu.VMEM((512, 256), F32),
            pltpu.VMEM((512, 256), F32),
            pltpu.VMEM((8, 64, 256), F32),
            pltpu.VMEM((1024, 256), BF16),
            pltpu.VMEM((1024, 1024), BF16),
            pltpu.VMEM((896, 256), F32),
        ]
        + [pltpu.VMEM((1024, w), F32) for w in WIDTHS]
        + [pltpu.VMEM((1024, w), BF16) for w in WIDTHS]
        + [pltpu.VMEM((128, w), F32) for w in WIDTHS]
        + [pltpu.VMEM((4, 32, w), F32) for w in WIDTHS]
        + [pltpu.VMEM((8, 128, w), BF16) for w in WIDTHS]
        + [pltpu.VMEM((8, 128, w), BF16) for w in WIDTHS]
        + [
            pltpu.SemaphoreType.DMA((len(MESSAGES),)),
            pltpu.SemaphoreType.DMA((len(MESSAGES),)),
            pltpu.SemaphoreType.DMA((2 + PARTS,)),
        ],
        compiler_params=pltpu.CompilerParams(
            collective_id=0, has_side_effects=True, vmem_limit_bytes=56 * 2**20
        ),
        cost_estimate=pl.CostEstimate(flops=3_800_000_000, bytes_accessed=4_000_000, transcendentals=0),
    )(example_ids.reshape(8, 128), activations, gradients, in_basis, out_basis)
    return squares / EXAMPLES


def solution(mesh):
    return jax.shard_map(
        shards,
        mesh=mesh,
        in_specs=(
            P(("tok", "ein"), "eout"),
            P("eout", ("tok", "ein")),
            P("eout", ("tok", "ein")),
            P(("tok", "ein"), "eout"),
            P(),
        ),
        out_specs=P(("tok", "ein"), "eout"),
        check_vma=False,
    )
```

```python
import jax
import jax.numpy as jnp
from jax import lax
from jax.experimental import pallas as pl
from jax.experimental.pallas import tpu as pltpu
from jax.sharding import PartitionSpec as P

EXAMPLES = 4
F32, BF16 = jnp.float32, jnp.bfloat16
MESH = pl.DeviceIdType.MESH
X, YL, YH, Z = 4, 2, 4, 8

WIDTHS = (256, 256, 256, 128)
HOPS = ((4, 3), (3, 4), (3, 4), (4, 3))
STARTS = tuple(sum(WIDTHS[:p]) for p in range(len(WIDTHS)))
PARTS = len(WIDTHS)
GRAD_HOPS = ((4, 3), (3, 4), (3, 4), (4, 3))
SIGN = (1, -1)

ORDER = (
    ("s",), ("fs", 4), ("g", 0, 0, 0), ("g", 0, 1, 0), ("fs", 5), ("fs", 3), ("fs", 7), ("fs", 2), ("g", 0, 0, 1),
    ("fs", 6), ("gy", 3), ("g", 1, 1, 0), ("g", 1, 0, 0), ("gy", 1), ("fs", 1), ("g", 3, 0, 0), ("g", 3, 1, 0),
    ("g", 0, 1, 1), ("f", 4), ("gy", 2), ("g", 2, 0, 0), ("g", 2, 1, 0), ("g", 0, 0, 2), ("m", 4), ("r", 1, 1, 0),
    ("r", 3, 0, 0), ("f", 5), ("g", 3, 0, 1), ("g", 1, 0, 1), ("fs", 0), ("r", 2, 1, 0), ("r", 0, 0, 0), ("f", 3),
    ("m", 5), ("r", 0, 1, 0), ("r", 3, 1, 0), ("m", 3), ("r", 3, 0, 1), ("r", 1, 0, 0), ("r", 1, 1, 1), ("f", 7),
    ("f", 2), ("r", 2, 0, 0), ("f", 6), ("r", 2, 1, 1), ("f", 1), ("g", 1, 1, 1), ("m", 2), ("r", 3, 0, 2), ("m", 6),
    ("r", 3, 1, 1), ("r", 1, 0, 1), ("r", 1, 1, 2), ("f", 0), ("r", 0, 0, 1), ("m", 7), ("r", 2, 1, 2),
    ("r", 2, 0, 1), ("g", 2, 1, 1), ("m", 1), ("r", 3, 0, 3), ("m", 0), ("r", 3, 1, 2), ("r", 1, 0, 2),
    ("r", 1, 1, 3), ("r", 0, 1, 1), ("g", 1, 1, 2), ("r", 0, 0, 2), ("r", 2, 1, 3), ("r", 2, 0, 2), ("g", 2, 1, 2),
    ("g", 1, 0, 2), ("g", 3, 1, 1), ("g", 2, 0, 1), ("g", 3, 0, 2), ("rf", 3), ("rf", 1), ("r", 0, 1, 2),
    ("g", 0, 1, 2), ("r", 0, 0, 3), ("g", 0, 0, 3), ("y", 3), ("rf", 2), ("g", 1, 1, 3), ("g", 2, 1, 3),
    ("g", 1, 0, 3), ("g", 2, 0, 2), ("g", 3, 0, 3), ("g", 3, 1, 2), ("rf", 0), ("w", 3), ("a", 3, 1, 0),
    ("g", 0, 1, 3), ("g", 1, 1, 4), ("g", 2, 0, 3), ("a", 3, 0, 0), ("g", 0, 0, 4), ("y", 1), ("g", 3, 0, 4),
    ("g", 2, 1, 4), ("g", 3, 1, 3), ("o",), ("y", 2), ("a", 3, 1, 1), ("a", 3, 0, 1), ("y", 0), ("c1",), ("w", 1),
    ("a", 1, 0, 0), ("a", 1, 1, 0), ("w", 2), ("a", 2, 1, 0), ("a", 2, 0, 0), ("w", 0), ("a", 0, 0, 0),
    ("a", 0, 1, 0), ("a", 3, 0, 2), ("a", 1, 1, 1), ("a", 2, 0, 1), ("a", 2, 1, 1), ("a", 3, 1, 2), ("a", 0, 1, 1),
    ("a", 0, 0, 1), ("a", 1, 0, 1), ("c2",), ("a", 1, 1, 2), ("a", 3, 0, 3), ("a", 2, 1, 2), ("a", 0, 0, 2),
    ("c3", 2), ("c3", 3), ("a", 1, 0, 2), ("c3", 4), ("a", 1, 1, 3), ("c3", 5), ("a", 0, 1, 2), ("c3", 1), ("c3", 6),
    ("c3", 7), ("a", 0, 0, 3), ("a", 2, 1, 3), ("a", 2, 0, 2), ("c4",), ("af", 3), ("af", 1), ("af", 0), ("af", 2),
)

MESSAGES = (
    [("f", i) for i in range(8)]
    + [("k", i) for i in range(8)]
    + [("gy", k) for k in range(1, 4)]
    + [("g", r, d, s) for r in range(4) for d in range(2) for s in range(GRAD_HOPS[r][d])]
    + [("sw",)]
    + [("d", j) for j in range(1, 8)]
    + [("cg", j) for j in range(1, 8)]
    + [("ck", j) for j in range(8)]
    + [("r", p, d, s) for p in range(PARTS) for d in range(2) for s in range(HOPS[p][d])]
    + [("yr", p, k) for p in range(PARTS) for k in range(1, 4)]
    + [("ya", p, k) for p in range(PARTS) for k in range(1, 4)]
    + [("a", p, d, s) for p in range(PARTS) for d in range(2) for s in range(HOPS[p][d])]
)
NUMBER = {name: i for i, name in enumerate(MESSAGES)}
FIRST = next(step[1] for step in ORDER if step[0] == "m")
LAG = 12


def rows(start, size):
    return pl.ds(pl.multiple_of(start, size), size)


def kernel(ids, act, grad, wi_hbm, wo_hbm, out_hbm, A, W, G, WO, PO, PR, PS, PQ, RO, MT, OUT, *rest):
    PI, R, YS = rest[0:PARTS], rest[PARTS : 2 * PARTS], rest[2 * PARTS : 3 * PARTS]
    YR, ZS, ZR = rest[3 * PARTS : 4 * PARTS], rest[4 * PARTS : 5 * PARTS], rest[5 * PARTS : 6 * PARTS]
    send_sem, recv_sem, local_sem = rest[6 * PARTS :]

    c = lax.axis_index("tok")
    e = lax.axis_index("ein")
    o = lax.axis_index("eout")
    x, yl = e % X, e // X
    z, yh = o % Z, o // Z

    known = {}

    def dev(dx=0, dyl=0, dyh=0, dz=0, dc=0):
        key = (dx, dyl, dyh, dz, dc)
        if key not in known:
            chip_in = (yl + dyl) % YL * X + (x + X + dx) % X if dx or dyl else e
            chip_out = (yh + dyh) % YH * Z + (z + Z + dz) % Z if dyh or dz else o
            known[key] = (1 - c if dc else c, chip_in, chip_out)
        return known[key]

    def te(dx=0, dyl=0, dc=0):
        return (c + dc) % 2 * 8 + (yl + dyl) % YL * X + (x + X + dx) % X

    load_wi = pltpu.make_async_copy(wi_hbm, W, local_sem.at[0])
    load_wo = pltpu.make_async_copy(wo_hbm, WO, local_sem.at[1])
    load_wi.start()
    load_wo.start()

    barrier = pltpu.get_barrier_semaphore()
    partners = [dev(dc=1), dev(dz=1), dev(dz=-1)]
    partners += [dev(dyh=k) for k in range(1, YH)]
    partners += [dev(dx=j % 4, dyl=j // 4) for j in range(1, 8)]
    for partner in partners:
        pl.semaphore_signal(barrier, 1, device_id=partner, device_id_type=MESH)
    pl.semaphore_wait(barrier, len(partners))

    flying = {}
    unsent = []
    step_number = [0]

    def send(name, src, dst, to):
        m = NUMBER[name]
        copy = pltpu.make_async_remote_copy(
            src_ref=src,
            dst_ref=dst,
            send_sem=send_sem.at[m],
            recv_sem=recv_sem.at[m],
            device_id=to,
            device_id_type=MESH,
        )
        copy.start()
        flying[name] = copy
        unsent.append((step_number[0], copy))

    def arrived(name):
        flying.pop(name).wait_recv()

    def chunk_of(i):
        return (z + i) % Z

    def block_copy(i):
        j = chunk_of(i)
        m = NUMBER["f", i]
        return pltpu.make_async_remote_copy(
            src_ref=act,
            dst_ref=A.at[j, c],
            send_sem=send_sem.at[m],
            recv_sem=recv_sem.at[m],
            device_id=(c, (yl + j // X) % YL * X + (x + X - j % X) % X, o),
            device_id_type=MESH,
        )

    def core_copy(i, j, src):
        m = NUMBER["k", 0] + i
        return pltpu.make_async_remote_copy(
            src_ref=src,
            dst_ref=A.at[j, c],
            send_sem=send_sem.at[m],
            recv_sem=recv_sem.at[m],
            device_id=dev(dc=1),
            device_id_type=MESH,
        )

    def step_s():
        core_copy((Z - z) % Z, 0, act).start()
        for k in (1, 3, 2):
            send(("gy", k), grad, G.at[o], dev(dyh=k))
        A[0, c] = act[...]
        G[o] = grad[...]

    def wait_block(i):
        @pl.when(chunk_of(i) != 0)
        def _():
            block_copy(i).wait_send()

    def step_fs(i):
        @pl.when(chunk_of(i) != 0)
        def _():
            block_copy(i).start()

    def step_f(i):
        j = chunk_of(i)

        @pl.when(j != 0)
        def _():
            block_copy(i).wait_recv()
            core_copy(i, j, A.at[j, c]).start()

    def step_m(i):
        if i == FIRST:
            load_wi.wait()
        j = chunk_of(i)
        core_copy(i, j, A.at[j, c]).wait_recv()
        lhs = A[j].reshape(128, 896)
        for p in range(PARTS):
            PI[p][j] = jnp.dot(lhs, W[:, STARTS[p] : STARTS[p] + WIDTHS[p]], preferred_element_type=F32)

    def step_gy(k):
        arrived(("gy", k))

    def step_g(r, d, s):
        if s > 0:
            arrived(("g", r, d, s - 1))
        if s < GRAD_HOPS[r][d]:
            j = (yh + r) % YH * Z + (z + Z - SIGN[d] * s) % Z
            send(("g", r, d, s), grad if r + s == 0 else G.at[j], G.at[j], dev(dz=SIGN[d]))

    def step_o():
        load_wo.wait()
        for h in range(4):
            PO[h * 256 : (h + 1) * 256, :] = jnp.dot(
                G[h * 8 : (h + 1) * 8].reshape(256, 512), WO[...], preferred_element_type=F32
            )
        send(("sw",), PO.at[rows((1 - c) * 512, 512)], PR, dev(dc=1))

    def step_c1():
        arrived(("sw",))
        PS[...] = PO[rows(c * 512, 512), :] + PR[...]
        for j in (4, 1, 3, 2, 5, 7, 6):
            to = (yl + j // 4) % YL * X + (x + j % 4) % X
            send(("d", j), PS.at[rows(to * 64, 64)], PQ.at[j], dev(dx=j % 4, dyl=j // 4))

    def step_c2():
        total = PS[rows(e * 64, 64), :]
        for j in range(1, 8):
            arrived(("d", j))
            total = total + PQ[j]
        mine = rows(te() * 64, 64)
        RO[mine, :] = total.astype(BF16)
        for j in (4, 1, 3, 2, 5, 7, 6):
            send(("cg", j), RO.at[mine], RO.at[mine], dev(dx=j % 4, dyl=j // 4))
        send(("ck", 0), RO.at[mine], RO.at[mine], dev(dc=1))

    def step_c3(j):
        arrived(("cg", j))
        b = RO.at[rows(te(dx=-(j % 4), dyl=j // 4) * 64, 64)]
        send(("ck", j), b, b, dev(dc=1))

    def step_c4():
        for j in range(8):
            arrived(("ck", j))
        low = lax.broadcasted_iota(jnp.int32, (1, 128), 1) < 64
        for j in range(8):
            at = (yl + j // X) % YL * X + (x + j % X) % X
            odd = at % 2 == 1
            first = ids[pl.ds(at // 2, 1), :]
            second = ids[pl.ds(4 + at // 2, 1), :]
            tokens = jnp.where(
                odd,
                jnp.where(low, pltpu.roll(first, 64, 1), second),
                jnp.where(low, first, pltpu.roll(second, 64, 1)),
            )
            block = jnp.concatenate([RO[rows(at * 64, 64), :], RO[rows(512 + at * 64, 64), :]], axis=0)
            block = block.astype(F32).T
            for n in range(EXAMPLES):
                MT[n * 256 : (n + 1) * 256, j * 128 : (j + 1) * 128] = jnp.where(
                    tokens == n, block, 0.0
                ).astype(BF16)

    def step_r(p, d, s):
        hops = HOPS[p][d]
        value = PI[p][(z + Z + SIGN[d] * (hops - s)) % Z]
        if s > 0:
            arrived(("r", p, d, s - 1))
            value = value + ZR[p][d * 4 + s - 1].astype(F32)
        ZS[p][d * 4 + s] = value.astype(BF16)
        send(("r", p, d, s), ZS[p].at[d * 4 + s], ZR[p].at[d * 4 + s], dev(dz=SIGN[d]))

    def step_rf(p):
        value = PI[p][z]
        for d in (0, 1):
            last = HOPS[p][d] - 1
            arrived(("r", p, d, last))
            value = value + ZR[p][d * 4 + last].astype(F32)
        YS[p][...] = value
        for k in (1, 3, 2):
            send(("yr", p, k), YS[p].at[rows((yh + k) % YH * 32, 32)], YR[p].at[k], dev(dyh=k))

    def step_y(p):
        value = YS[p][rows(yh * 32, 32), :]
        for k in (1, 2, 3):
            arrived(("yr", p, k))
            value = value + YR[p][k]
        R[p][z, rows(yh * 32, 32), :] = value.astype(BF16)
        mine = R[p].at[z, rows(yh * 32, 32)]
        for k in (1, 3, 2):
            send(("ya", p, k), mine, mine, dev(dyh=k))

    def step_w(p):
        for k in (1, 2, 3):
            arrived(("ya", p, k))

    def step_a(p, d, s):
        if s > 0:
            arrived(("a", p, d, s - 1))
        b = R[p].at[(z + Z - SIGN[d] * s) % Z]
        send(("a", p, d, s), b, b, dev(dz=SIGN[d]))

    def step_af(p):
        for d in (0, 1):
            arrived(("a", p, d, HOPS[p][d] - 1))
        rhs = R[p][...].reshape(1024, WIDTHS[p])
        total = None
        for n in range(EXAMPLES):
            tile = jnp.dot(MT[n * 256 : (n + 1) * 256, :], rhs, preferred_element_type=F32)
            total = tile * tile if total is None else total + tile * tile
        here = slice(STARTS[p], STARTS[p] + WIDTHS[p])
        OUT[here, :] = total.T
        copy = pltpu.make_async_copy(OUT.at[here], out_hbm.at[here], local_sem.at[2 + p])
        copy.start()
        stores.append(copy)

    stores = []
    steps = {
        "s": step_s, "fs": step_fs, "f": step_f, "m": step_m, "gy": step_gy, "g": step_g, "o": step_o, "c1": step_c1, "c2": step_c2,
        "c3": step_c3, "c4": step_c4, "r": step_r, "rf": step_rf, "y": step_y, "w": step_w, "a": step_a, "af": step_af,
    }
    for name, *which in ORDER:
        steps[name](*which)
        step_number[0] += 1
        while unsent and unsent[0][0] < step_number[0] - LAG:
            unsent.pop(0)[1].wait_send()
    for _, copy in unsent:
        copy.wait_send()
    for i in range(8):
        core_copy(i, 0, act).wait_send()
        wait_block(i)
    for copy in stores:
        copy.wait()


def shards(activations, gradients, in_basis, out_basis, example_ids):
    vmem, anywhere = pl.BlockSpec(memory_space=pltpu.VMEM), pl.BlockSpec(memory_space=pl.ANY)
    squares = pl.pallas_call(
        kernel,
        out_shape=jax.ShapeDtypeStruct((896, 256), F32),
        in_specs=[vmem, vmem, vmem, anywhere, anywhere],
        out_specs=anywhere,
        scratch_shapes=[
            pltpu.VMEM((8, 2, 64, 896), BF16),
            pltpu.VMEM((896, 896), BF16),
            pltpu.VMEM((32, 32, 512), BF16),
            pltpu.VMEM((512, 256), BF16),
            pltpu.VMEM((1024, 256), F32),
            pltpu.VMEM((512, 256), F32),
            pltpu.VMEM((512, 256), F32),
            pltpu.VMEM((8, 64, 256), F32),
            pltpu.VMEM((1024, 256), BF16),
            pltpu.VMEM((1024, 1024), BF16),
            pltpu.VMEM((896, 256), F32),
        ]
        + [pltpu.VMEM((8, 128, w), F32) for w in WIDTHS]
        + [pltpu.VMEM((8, 128, w), BF16) for w in WIDTHS]
        + [pltpu.VMEM((128, w), F32) for w in WIDTHS]
        + [pltpu.VMEM((4, 32, w), F32) for w in WIDTHS]
        + [pltpu.VMEM((8, 128, w), BF16) for w in WIDTHS]
        + [pltpu.VMEM((8, 128, w), BF16) for w in WIDTHS]
        + [
            pltpu.SemaphoreType.DMA((len(MESSAGES),)),
            pltpu.SemaphoreType.DMA((len(MESSAGES),)),
            pltpu.SemaphoreType.DMA((2 + PARTS,)),
        ],
        compiler_params=pltpu.CompilerParams(
            collective_id=0, has_side_effects=True, vmem_limit_bytes=56 * 2**20
        ),
        cost_estimate=pl.CostEstimate(flops=3_800_000_000, bytes_accessed=4_000_000, transcendentals=0),
    )(example_ids.reshape(8, 128), activations, gradients, in_basis, out_basis)
    return squares / EXAMPLES


def solution(mesh):
    return jax.shard_map(
        shards,
        mesh=mesh,
        in_specs=(
            P(("tok", "ein"), "eout"),
            P("eout", ("tok", "ein")),
            P("eout", ("tok", "ein")),
            P(("tok", "ein"), "eout"),
            P(),
        ),
        out_specs=P(("tok", "ein"), "eout"),
        check_vma=False,
    )
```

```python
import jax
import jax.numpy as jnp
from jax import lax
from jax.experimental import pallas as pl
from jax.experimental.pallas import tpu as pltpu
from jax.sharding import PartitionSpec as P

EXAMPLES = 4
F32, BF16 = jnp.float32, jnp.bfloat16
MESH = pl.DeviceIdType.MESH
X, YL, YH, Z = 4, 2, 4, 8

WIDTHS = (256, 256, 128, 256)
HOPS = ((4, 3), (3, 4), (4, 3), (3, 4))
STARTS = tuple(sum(WIDTHS[:p]) for p in range(len(WIDTHS)))
PARTS = len(WIDTHS)
GRAD_HOPS = ((4, 3), (3, 4), (3, 4), (4, 3))
SIGN = (1, -1)

ORDER = (
    ("s",), ("g", 0, 0, 0), ("fs", 4), ("g", 0, 1, 0), ("fs", 5), ("fs", 3), ("fs", 1), ("fs", 6), ("g", 0, 0, 1),
    ("gy", 3), ("g", 1, 1, 0), ("fs", 7), ("g", 0, 1, 1), ("g", 1, 0, 0), ("fs", 2), ("gy", 1), ("g", 3, 0, 0),
    ("g", 3, 1, 0), ("f", 4), ("gy", 2), ("g", 2, 1, 0), ("g", 2, 0, 0), ("fs", 0), ("g", 0, 0, 2), ("g", 1, 0, 1),
    ("g", 1, 1, 1), ("m", 4), ("r", 2, 0, 0), ("f", 5), ("r", 0, 0, 0), ("r", 1, 1, 0), ("r", 3, 1, 0),
    ("g", 3, 0, 1), ("g", 2, 1, 1), ("f", 1), ("g", 2, 0, 1), ("f", 3), ("m", 5), ("r", 2, 1, 0), ("r", 0, 1, 0),
    ("m", 3), ("r", 2, 0, 1), ("f", 6), ("r", 0, 0, 1), ("g", 3, 1, 1), ("f", 2), ("r", 1, 0, 0), ("r", 3, 0, 0),
    ("r", 1, 1, 1), ("f", 7), ("m", 6), ("r", 2, 1, 1), ("m", 2), ("r", 0, 1, 1), ("r", 2, 0, 2), ("f", 0),
    ("r", 0, 0, 2), ("r", 3, 1, 1), ("m", 7), ("r", 1, 0, 1), ("r", 2, 1, 2), ("r", 1, 1, 2), ("m", 1),
    ("r", 2, 0, 3), ("r", 0, 1, 2), ("r", 0, 0, 3), ("r", 3, 0, 1), ("r", 3, 1, 2), ("m", 0), ("g", 1, 1, 2),
    ("r", 1, 0, 2), ("rf", 2), ("r", 1, 1, 3), ("g", 2, 1, 2), ("g", 2, 0, 2), ("g", 3, 0, 2), ("rf", 0),
    ("r", 3, 1, 3), ("r", 3, 0, 2), ("g", 1, 1, 3), ("g", 0, 0, 3), ("g", 0, 1, 2), ("g", 1, 0, 2), ("g", 3, 1, 2),
    ("y", 2), ("rf", 1), ("g", 2, 1, 3), ("g", 2, 0, 3), ("g", 3, 0, 3), ("rf", 3), ("y", 0), ("g", 0, 0, 4),
    ("g", 1, 1, 4), ("w", 2), ("a", 2, 1, 0), ("g", 1, 0, 3), ("g", 0, 1, 3), ("a", 2, 0, 0), ("g", 3, 1, 3),
    ("g", 3, 0, 4), ("g", 2, 1, 4), ("o",), ("y", 1), ("a", 2, 1, 1), ("a", 2, 0, 1), ("y", 3), ("c1",), ("w", 0),
    ("a", 0, 1, 0), ("a", 0, 0, 0), ("w", 1), ("a", 1, 1, 0), ("a", 2, 0, 2), ("a", 1, 0, 0), ("w", 3),
    ("a", 3, 1, 0), ("a", 0, 0, 1), ("a", 2, 1, 2), ("a", 3, 0, 0), ("a", 1, 1, 1), ("a", 3, 1, 1), ("a", 1, 0, 1),
    ("a", 0, 1, 1), ("a", 2, 0, 3), ("c2",), ("a", 0, 0, 2), ("a", 1, 1, 2), ("a", 3, 0, 1), ("a", 3, 1, 2),
    ("a", 1, 0, 2), ("a", 0, 1, 2), ("c3", 1), ("c3", 2), ("c3", 4), ("c3", 3), ("a", 0, 0, 3), ("c3", 5), ("c3", 7),
    ("c3", 6), ("a", 1, 1, 3), ("a", 3, 0, 2), ("a", 3, 1, 3), ("c4",), ("af", 2), ("af", 0), ("af", 1), ("af", 3),
)

MESSAGES = (
    [("f", i) for i in range(8)]
    + [("k", i) for i in range(8)]
    + [("gy", k) for k in range(1, 4)]
    + [("g", r, d, s) for r in range(4) for d in range(2) for s in range(GRAD_HOPS[r][d])]
    + [("sw",)]
    + [("d", j) for j in range(1, 8)]
    + [("cg", j) for j in range(1, 8)]
    + [("ck", j) for j in range(8)]
    + [("r", p, d, s) for p in range(PARTS) for d in range(2) for s in range(HOPS[p][d])]
    + [("yr", p, k) for p in range(PARTS) for k in range(1, 4)]
    + [("ya", p, k) for p in range(PARTS) for k in range(1, 4)]
    + [("a", p, d, s) for p in range(PARTS) for d in range(2) for s in range(HOPS[p][d])]
)
NUMBER = {name: i for i, name in enumerate(MESSAGES)}
FIRST = next(step[1] for step in ORDER if step[0] == "m")
LAG = 12


def rows(start, size):
    return pl.ds(pl.multiple_of(start, size), size)


def kernel(ids, act, grad, wi_hbm, wo_hbm, out_hbm, A, W, G, WO, PO, PR, PS, PQ, RO, MT, OUT, *rest):
    PI, R, YS = rest[0:PARTS], rest[PARTS : 2 * PARTS], rest[2 * PARTS : 3 * PARTS]
    YR, ZS, ZR = rest[3 * PARTS : 4 * PARTS], rest[4 * PARTS : 5 * PARTS], rest[5 * PARTS : 6 * PARTS]
    send_sem, recv_sem, local_sem = rest[6 * PARTS :]

    c = lax.axis_index("tok")
    e = lax.axis_index("ein")
    o = lax.axis_index("eout")
    x, yl = e % X, e // X
    z, yh = o % Z, o // Z

    known = {}

    def dev(dx=0, dyl=0, dyh=0, dz=0, dc=0):
        key = (dx, dyl, dyh, dz, dc)
        if key not in known:
            chip_in = (yl + dyl) % YL * X + (x + X + dx) % X if dx or dyl else e
            chip_out = (yh + dyh) % YH * Z + (z + Z + dz) % Z if dyh or dz else o
            known[key] = (1 - c if dc else c, chip_in, chip_out)
        return known[key]

    def te(dx=0, dyl=0, dc=0):
        return (c + dc) % 2 * 8 + (yl + dyl) % YL * X + (x + X + dx) % X

    load_wi = pltpu.make_async_copy(wi_hbm, W, local_sem.at[0])
    load_wo = pltpu.make_async_copy(wo_hbm, WO, local_sem.at[1])
    load_wi.start()
    load_wo.start()

    barrier = pltpu.get_barrier_semaphore()
    partners = [dev(dc=1), dev(dz=1), dev(dz=-1)]
    partners += [dev(dyh=k) for k in range(1, YH)]
    partners += [dev(dx=j % 4, dyl=j // 4) for j in range(1, 8)]
    for partner in partners:
        pl.semaphore_signal(barrier, 1, device_id=partner, device_id_type=MESH)
    pl.semaphore_wait(barrier, len(partners))

    flying = {}
    unsent = []
    step_number = [0]

    def send(name, src, dst, to):
        m = NUMBER[name]
        copy = pltpu.make_async_remote_copy(
            src_ref=src,
            dst_ref=dst,
            send_sem=send_sem.at[m],
            recv_sem=recv_sem.at[m],
            device_id=to,
            device_id_type=MESH,
        )
        copy.start()
        flying[name] = copy
        unsent.append((step_number[0], copy))

    def arrived(name):
        flying.pop(name).wait_recv()

    def chunk_of(i):
        return (z + i) % Z

    def block_copy(i):
        j = chunk_of(i)
        m = NUMBER["f", i]
        return pltpu.make_async_remote_copy(
            src_ref=act,
            dst_ref=A.at[j, c],
            send_sem=send_sem.at[m],
            recv_sem=recv_sem.at[m],
            device_id=(c, (yl + j // X) % YL * X + (x + X - j % X) % X, o),
            device_id_type=MESH,
        )

    def core_copy(i, j, src):
        m = NUMBER["k", 0] + i
        return pltpu.make_async_remote_copy(
            src_ref=src,
            dst_ref=A.at[j, c],
            send_sem=send_sem.at[m],
            recv_sem=recv_sem.at[m],
            device_id=dev(dc=1),
            device_id_type=MESH,
        )

    def step_s():
        core_copy((Z - z) % Z, 0, act).start()
        for k in (1, 3, 2):
            send(("gy", k), grad, G.at[o], dev(dyh=k))
        A[0, c] = act[...]
        G[o] = grad[...]

    def wait_block(i):
        @pl.when(chunk_of(i) != 0)
        def _():
            block_copy(i).wait_send()

    def step_fs(i):
        @pl.when(chunk_of(i) != 0)
        def _():
            block_copy(i).start()

    def step_f(i):
        j = chunk_of(i)

        @pl.when(j != 0)
        def _():
            block_copy(i).wait_recv()
            core_copy(i, j, A.at[j, c]).start()

    def step_m(i):
        if i == FIRST:
            load_wi.wait()
        j = chunk_of(i)
        core_copy(i, j, A.at[j, c]).wait_recv()
        lhs = A[j].reshape(128, 896)
        for p in range(PARTS):
            PI[p][j] = jnp.dot(lhs, W[:, STARTS[p] : STARTS[p] + WIDTHS[p]], preferred_element_type=F32)

    def step_gy(k):
        arrived(("gy", k))

    def step_g(r, d, s):
        if s > 0:
            arrived(("g", r, d, s - 1))
        if s < GRAD_HOPS[r][d]:
            j = (yh + r) % YH * Z + (z + Z - SIGN[d] * s) % Z
            send(("g", r, d, s), grad if r + s == 0 else G.at[j], G.at[j], dev(dz=SIGN[d]))

    def step_o():
        load_wo.wait()
        for h in range(4):
            PO[h * 256 : (h + 1) * 256, :] = jnp.dot(
                G[h * 8 : (h + 1) * 8].reshape(256, 512), WO[...], preferred_element_type=F32
            )
        send(("sw",), PO.at[rows((1 - c) * 512, 512)], PR, dev(dc=1))

    def step_c1():
        arrived(("sw",))
        PS[...] = PO[rows(c * 512, 512), :] + PR[...]
        for j in (4, 1, 3, 2, 5, 7, 6):
            to = (yl + j // 4) % YL * X + (x + j % 4) % X
            send(("d", j), PS.at[rows(to * 64, 64)], PQ.at[j], dev(dx=j % 4, dyl=j // 4))

    def step_c2():
        total = PS[rows(e * 64, 64), :]
        for j in range(1, 8):
            arrived(("d", j))
            total = total + PQ[j]
        mine = rows(te() * 64, 64)
        RO[mine, :] = total.astype(BF16)
        for j in (4, 1, 3, 2, 5, 7, 6):
            send(("cg", j), RO.at[mine], RO.at[mine], dev(dx=j % 4, dyl=j // 4))
        send(("ck", 0), RO.at[mine], RO.at[mine], dev(dc=1))

    def step_c3(j):
        arrived(("cg", j))
        b = RO.at[rows(te(dx=-(j % 4), dyl=j // 4) * 64, 64)]
        send(("ck", j), b, b, dev(dc=1))

    def step_c4():
        for j in range(8):
            arrived(("ck", j))
        low = lax.broadcasted_iota(jnp.int32, (1, 128), 1) < 64
        for j in range(8):
            at = (yl + j // X) % YL * X + (x + j % X) % X
            odd = at % 2 == 1
            first = ids[pl.ds(at // 2, 1), :]
            second = ids[pl.ds(4 + at // 2, 1), :]
            tokens = jnp.where(
                odd,
                jnp.where(low, pltpu.roll(first, 64, 1), second),
                jnp.where(low, first, pltpu.roll(second, 64, 1)),
            )
            block = jnp.concatenate([RO[rows(at * 64, 64), :], RO[rows(512 + at * 64, 64), :]], axis=0)
            block = block.astype(F32).T
            for n in range(EXAMPLES):
                MT[n * 256 : (n + 1) * 256, j * 128 : (j + 1) * 128] = jnp.where(
                    tokens == n, block, 0.0
                ).astype(BF16)

    def step_r(p, d, s):
        hops = HOPS[p][d]
        value = PI[p][(z + Z + SIGN[d] * (hops - s)) % Z]
        if s > 0:
            arrived(("r", p, d, s - 1))
            value = value + ZR[p][d * 4 + s - 1].astype(F32)
        ZS[p][d * 4 + s] = value.astype(BF16)
        send(("r", p, d, s), ZS[p].at[d * 4 + s], ZR[p].at[d * 4 + s], dev(dz=SIGN[d]))

    def step_rf(p):
        value = PI[p][z]
        for d in (0, 1):
            last = HOPS[p][d] - 1
            arrived(("r", p, d, last))
            value = value + ZR[p][d * 4 + last].astype(F32)
        YS[p][...] = value
        for k in (1, 3, 2):
            send(("yr", p, k), YS[p].at[rows((yh + k) % YH * 32, 32)], YR[p].at[k], dev(dyh=k))

    def step_y(p):
        value = YS[p][rows(yh * 32, 32), :]
        for k in (1, 2, 3):
            arrived(("yr", p, k))
            value = value + YR[p][k]
        R[p][z, rows(yh * 32, 32), :] = value.astype(BF16)
        mine = R[p].at[z, rows(yh * 32, 32)]
        for k in (1, 3, 2):
            send(("ya", p, k), mine, mine, dev(dyh=k))

    def step_w(p):
        for k in (1, 2, 3):
            arrived(("ya", p, k))

    def step_a(p, d, s):
        if s > 0:
            arrived(("a", p, d, s - 1))
        b = R[p].at[(z + Z - SIGN[d] * s) % Z]
        send(("a", p, d, s), b, b, dev(dz=SIGN[d]))

    def step_af(p):
        for d in (0, 1):
            arrived(("a", p, d, HOPS[p][d] - 1))
        rhs = R[p][...].reshape(1024, WIDTHS[p])
        total = None
        for n in range(EXAMPLES):
            tile = jnp.dot(MT[n * 256 : (n + 1) * 256, :], rhs, preferred_element_type=F32)
            total = tile * tile if total is None else total + tile * tile
        here = slice(STARTS[p], STARTS[p] + WIDTHS[p])
        OUT[here, :] = total.T
        copy = pltpu.make_async_copy(OUT.at[here], out_hbm.at[here], local_sem.at[2 + p])
        copy.start()
        stores.append(copy)

    stores = []
    steps = {
        "s": step_s, "fs": step_fs, "f": step_f, "m": step_m, "gy": step_gy, "g": step_g, "o": step_o, "c1": step_c1, "c2": step_c2,
        "c3": step_c3, "c4": step_c4, "r": step_r, "rf": step_rf, "y": step_y, "w": step_w, "a": step_a, "af": step_af,
    }
    for name, *which in ORDER:
        steps[name](*which)
        step_number[0] += 1
        while unsent and unsent[0][0] < step_number[0] - LAG:
            unsent.pop(0)[1].wait_send()
    for _, copy in unsent:
        copy.wait_send()
    for i in range(8):
        core_copy(i, 0, act).wait_send()
        wait_block(i)
    for copy in stores:
        copy.wait()


def shards(activations, gradients, in_basis, out_basis, example_ids):
    vmem, anywhere = pl.BlockSpec(memory_space=pltpu.VMEM), pl.BlockSpec(memory_space=pl.ANY)
    squares = pl.pallas_call(
        kernel,
        out_shape=jax.ShapeDtypeStruct((896, 256), F32),
        in_specs=[vmem, vmem, vmem, anywhere, anywhere],
        out_specs=anywhere,
        scratch_shapes=[
            pltpu.VMEM((8, 2, 64, 896), BF16),
            pltpu.VMEM((896, 896), BF16),
            pltpu.VMEM((32, 32, 512), BF16),
            pltpu.VMEM((512, 256), BF16),
            pltpu.VMEM((1024, 256), F32),
            pltpu.VMEM((512, 256), F32),
            pltpu.VMEM((512, 256), F32),
            pltpu.VMEM((8, 64, 256), F32),
            pltpu.VMEM((1024, 256), BF16),
            pltpu.VMEM((1024, 1024), BF16),
            pltpu.VMEM((896, 256), F32),
        ]
        + [pltpu.VMEM((8, 128, w), F32) for w in WIDTHS]
        + [pltpu.VMEM((8, 128, w), BF16) for w in WIDTHS]
        + [pltpu.VMEM((128, w), F32) for w in WIDTHS]
        + [pltpu.VMEM((4, 32, w), F32) for w in WIDTHS]
        + [pltpu.VMEM((8, 128, w), BF16) for w in WIDTHS]
        + [pltpu.VMEM((8, 128, w), BF16) for w in WIDTHS]
        + [
            pltpu.SemaphoreType.DMA((len(MESSAGES),)),
            pltpu.SemaphoreType.DMA((len(MESSAGES),)),
            pltpu.SemaphoreType.DMA((2 + PARTS,)),
        ],
        compiler_params=pltpu.CompilerParams(
            collective_id=0, has_side_effects=True, vmem_limit_bytes=56 * 2**20
        ),
        cost_estimate=pl.CostEstimate(flops=3_800_000_000, bytes_accessed=4_000_000, transcendentals=0),
    )(example_ids.reshape(8, 128), activations, gradients, in_basis, out_basis)
    return squares / EXAMPLES


def solution(mesh):
    return jax.shard_map(
        shards,
        mesh=mesh,
        in_specs=(
            P(("tok", "ein"), "eout"),
            P("eout", ("tok", "ein")),
            P("eout", ("tok", "ein")),
            P(("tok", "ein"), "eout"),
            P(),
        ),
        out_specs=P(("tok", "ein"), "eout"),
        check_vma=False,
    )
```
